128 devices in a mesh: rep: 2 (over x_lo), row: 64 (over y, x_hi, z, core).
Axes of the slice: x: 4 (x_hi: 2, x_lo: 2; x = x_hi * 2 + x_lo), y: 4, z: 4, core: 2. Of those that a mesh axis runs over, the one named last changes fastest.
Arguments:
- features: bfloat16 [65536, 256], P(('rep', 'row')), may hold values from -6 to 6
- tile_vals: bfloat16 [90112, 128, 128], P(('rep', 'row')), may hold values from 0 to 1, as said below
- tile_dst: int32 [90112], P(('rep', 'row')), may hold values from 0 to 7
- tile_src: int32 [90112], P(('rep', 'row')), may hold values from 0 to 255, as said below
- tile_count: int32 [128], P(('rep', 'row')), may hold values from 88 to 704
- degree: int32 [65536], P(('rep', 'row')), may hold values from 88 to 703
- w_self: bfloat16 [256, 256], replicated, may hold values from -0.375 to 0.375
- w_neigh: bfloat16 [256, 256], replicated, may hold values from -0.375 to 0.375
- out_bias: float32 [256], replicated, may hold values from -4 to 4
Outputs:
- result: bfloat16 [65536, 256], P(('rep', 'row'))
The draws below stay inside these ranges and needn't reach their ends.
Inputs may be any that keep to these rules, and one draw needn't show every extreme that they name: Within each device's live slots the pairs (tile_src, tile_dst) are distinct and in ascending order of tile_src, then tile_dst. `tile_vals`: entries are 0 or 1.
All inputs are finite; a program needn't handle non-finite values.
Results may differ from the reference program's by a relative error of at most 0.0028.
Values may be sent and summed in bfloat16 or wider, within the bound.
No kernel may reach another device: no remote copies, remote signals or barrier semaphores. Data moves between devices by JAX's collectives and lax.ppermute only.
A program may use at most 128 MiB of HBM per device.

```python
import jax
import jax.numpy as jnp
from jax import lax

H = 256
BLOCK = 128
NB_DEV = 4
TILES_DEV = 704
SRC_BLOCKS = 256
NODES = 65536
DEG_LO = 352
N_REP = 2
N_ROW = 64


def tile_layout(key):
    device_total = N_REP * N_ROW
    pair_total = 2 * NB_DEV * SRC_BLOCKS
    raw_draw = jax.random.randint(jax.random.fold_in(key, 101), (device_total,), 0, TILES_DEV + 1)
    counts = jnp.maximum(raw_draw * raw_draw // TILES_DEV, TILES_DEV // 8)
    busiest = jax.random.randint(jax.random.fold_in(key, 102), (), 0, device_total)
    counts = jnp.where(jnp.arange(device_total) == busiest, TILES_DEV, counts).astype(jnp.int32)
    base_key = jax.random.fold_in(key, 103)

    def per_device(device, live_tiles):
        chosen = jax.random.permutation(jax.random.fold_in(base_key, device), pair_total)[:TILES_DEV].astype(jnp.int32)
        slots = jnp.arange(TILES_DEV, dtype=jnp.int32)
        order_key = jnp.where(slots < live_tiles, chosen, chosen + pair_total)
        ranked = jnp.sort(order_key)
        return jnp.where(ranked >= pair_total, ranked - pair_total, ranked)
    pair_ids = jax.vmap(per_device)(jnp.arange(device_total, dtype=jnp.int32), counts)
    return (counts, pair_ids.reshape(-1).astype(jnp.int32))


def draw_tile_dst(key, part):
    counts, pair_ids = tile_layout(key)
    return (pair_ids % (2 * NB_DEV)).astype(jnp.int32)


def draw_tile_src(key, part):
    counts, pair_ids = tile_layout(key)
    return (pair_ids // (2 * NB_DEV)).astype(jnp.int32)


def draw_tile_count(key, part):
    counts, pair_ids = tile_layout(key)
    return counts.astype(jnp.int32)


def draw_tile_vals(key, part):
    key = jax.random.fold_in(key, 4)
    entries = jax.random.bernoulli(key, 2.0 / BLOCK, (N_REP * N_ROW * TILES_DEV, BLOCK, BLOCK))
    return entries.astype(jnp.float32).astype(jnp.bfloat16)


def with_ends(drawn, rng, least, high):
    longest = drawn.shape.index(max(drawn.shape))
    spots = []
    for shift in (0, 1):
        where = [jax.random.randint(jax.random.fold_in(rng, axis), (), 0, length) for axis, length in enumerate(drawn.shape)]
        where[longest] = (where[longest] + shift) % drawn.shape[longest]
        spots.append(tuple(where))
    return drawn.at[spots[0]].set(least).at[spots[1]].set(high)


def block_levels(own_key, dims, split, least, high):
    def one(axis_at, parts):
        heights = jax.random.uniform(jax.random.fold_in(jax.random.fold_in(own_key, 6), axis_at), (parts,), jnp.float32, least / len(split), high / len(split))
        return jnp.repeat(jnp.exp(heights), dims[axis_at] // parts).reshape((-1,) + (1,) * (len(dims) - axis_at - 1))

    loudness = one(*split[0])
    for cut in split[1:]:
        loudness = loudness * one(*cut)
    return loudness


def gaussian(rng, shape, deviation, bound, cuts=(), kind=jnp.bfloat16):
    result = deviation * jax.random.normal(rng, shape, jnp.float32)
    if cuts:
        result = result * block_levels(rng, shape, cuts, -0.22, 0.18)
    return jnp.clip(result, -bound, bound).astype(kind)


def setup_inputs(seed: int = 0) -> dict:
    splits = jax.random.split(jax.random.key(seed), 10)
    features = gaussian(splits[0], (NODES, H), 1.0, 6.0, ((0, 128),))
    tile_vals = draw_tile_vals(jax.random.fold_in(splits[9], 71), 0)
    tile_dst = draw_tile_dst(jax.random.fold_in(splits[9], 71), 0)
    tile_src = draw_tile_src(jax.random.fold_in(splits[9], 71), 0)
    tile_count = draw_tile_count(jax.random.fold_in(splits[9], 71), 0)
    degree = with_ends(jax.random.randint(splits[5], (NODES,), DEG_LO // 4, 2 * DEG_LO), jax.random.fold_in(splits[5], 1), DEG_LO // 4, (2 * DEG_LO) - 1).astype(jnp.int32)
    w_self = gaussian(splits[6], (H, H), H ** -0.5, 0.375)
    w_neigh = gaussian(splits[7], (H, H), H ** -0.5, 0.375)
    out_bias = gaussian(splits[8], (H,), 1.0, 4.0, (), jnp.float32)
    return dict(features=features, tile_vals=tile_vals, tile_dst=tile_dst, tile_src=tile_src, tile_count=tile_count, degree=degree, w_self=w_self, w_neigh=w_neigh, out_bias=out_bias)


def pick_step(tile_total):
    for candidate in (64, 32, 16, 8, 4):
        if tile_total % candidate == 0:
            return candidate
    return tile_total

def reference(features, tile_vals, tile_dst, tile_src, tile_count, degree, w_self, w_neigh, out_bias):
    feat_width = features.shape[1]
    block_total = NODES // BLOCK
    source_all = features.reshape(block_total, BLOCK, feat_width).astype(jnp.float32)
    device_total = N_REP * N_ROW
    tile_step = pick_step(TILES_DEV)
    turn_total = TILES_DEV // tile_step

    def per_device(aggregate, device):
        replica = device // N_ROW
        row_pos = device % N_ROW
        live_tiles = tile_count[device]
        base = (device * TILES_DEV).astype(jnp.int32)

        def per_turn(running, turn_index):
            start = (base + turn_index * tile_step).astype(jnp.int32)
            tile_block = lax.dynamic_slice_in_dim(tile_vals, start, tile_step, 0).astype(jnp.float32)
            dst_block = lax.dynamic_slice_in_dim(tile_dst, start, tile_step, 0)
            src_block = lax.dynamic_slice_in_dim(tile_src, start, tile_step, 0)
            slot_ids = turn_index * tile_step + jnp.arange(tile_step, dtype=jnp.int32)
            live_mask = slot_ids < live_tiles
            rows_at = (dst_block // NB_DEV * N_ROW + row_pos) * NB_DEV + dst_block % NB_DEV
            cols_at = replica * SRC_BLOCKS + src_block
            products = jnp.einsum('tij,tjh->tih', tile_block, source_all[cols_at])
            products = jnp.where(live_mask[:, None, None], products, jnp.zeros_like(products))
            return (running.at[rows_at].add(products), None)
        aggregate, _ = lax.scan(per_turn, aggregate, jnp.arange(turn_total, dtype=jnp.int32))
        return (aggregate, None)
    empty_sum = jnp.zeros((block_total, BLOCK, feat_width), jnp.float32)
    aggregate, _ = lax.scan(per_device, empty_sum, jnp.arange(device_total, dtype=jnp.int32))
    aggregate = aggregate.reshape(NODES, feat_width)
    neighbours = (aggregate / jnp.sqrt(degree.astype(jnp.float32))[:, None]).astype(jnp.bfloat16)
    mixed = jnp.dot(features, w_self, preferred_element_type=jnp.float32)
    mixed = mixed + jnp.dot(neighbours, w_neigh, preferred_element_type=jnp.float32)
    mixed = mixed + out_bias.astype(jnp.float32)[None, :]
    return jnp.maximum(mixed, 0.0).astype(jnp.bfloat16)
```

```python
import functools

import jax
import jax.numpy as jnp
from jax import lax
from jax.experimental import pallas as pl
from jax.experimental.pallas import tpu as pltpu
from jax.sharding import PartitionSpec as P

Y, X, Z, C = 4, 2, 4, 2
DEV_ROWS = 512
DEV_BLOCKS = 4
DSTS = 8
STEP = 2 * DSTS
SRC_BITS = 9
ZERO_BLOCK = 256
RING = 6
PHASE_STEPS = (48, 32, 32, 16)
PHASE_BASE = tuple(STEP * sum(PHASE_STEPS[:i]) for i in range(4))
SLOTS = STEP * sum(PHASE_STEPS)
LINE = (0, -1, 1, 2)


def row_id(y, x, z, c):
    return ((y % Y * X + x % X) * Z + z % Z) * C + c % C


def shift(y=(0, 0), x=0, z=(0, 0), c=0):
    return [
        (row_id(i, j, k, m), row_id(i + y[m], j + x, k + z[m], m + c))
        for i in range(Y) for j in range(X) for k in range(Z) for m in range(C)
    ]


def along_first(step):
    return shift(y=(step, 0), z=(0, step))


def along_second(step):
    return shift(y=(0, step), z=(step, 0))


def send(rows, pairs):
    return lax.ppermute(rows, "row", pairs)


def line_of(plane, second, places=LINE):
    return [(plane, first, second) for first in places]


def own_pieces(features):
    head, tail = LINE[:2], LINE[2:]
    from_minus = send(features, along_first(1))
    from_plus = send(features, along_first(-1))
    from_far = send(features, along_first(2))
    across = send(features, shift(x=1))
    from_minus, from_plus, from_far, across = lax.optimization_barrier(
        (from_minus, from_plus, from_far, across)
    )
    line = jnp.concatenate([features, from_minus, from_plus, from_far])
    minus = send(line, along_second(1))
    plus = send(line, along_second(-1))
    rest = send(line[DEV_ROWS:], shift(x=1))
    minus, plus = lax.optimization_barrier((minus, plus))
    far_head = send(minus[: 2 * DEV_ROWS], along_second(1))
    far_tail = send(plus[2 * DEV_ROWS :], along_second(-1))
    rest, _, _ = lax.optimization_barrier((rest, minus, plus))
    other = jnp.concatenate([across, rest])
    other_minus = send(other, along_second(1))
    other_plus = send(other, along_second(-1))
    other_head = send(other_minus[: 2 * DEV_ROWS], along_second(1))
    other_tail = send(other_plus[2 * DEV_ROWS :], along_second(-1))
    return (
        ((line, line_of(0, 0)), (minus, line_of(0, -1)), (plus, line_of(0, 1))),
        ((far_head, line_of(0, 2, head)), (far_tail, line_of(0, 2, tail)), (other, line_of(1, 0))),
        ((other_minus, line_of(1, -1)), (other_plus, line_of(1, 1))),
        ((other_head, line_of(1, 2, head)), (other_tail, line_of(1, 2, tail))),
    )


def owners(places, row, core):
    y, x, z = row // (X * Z * C), row // (Z * C) % X, row // C % Z
    found = []
    for plane, first, second in places:
        dy = jnp.where(core == 0, first, second)
        dz = jnp.where(core == 0, second, first)
        found.append(row_id(y + dy, x + plane, z + dz, core))
    return found


def phase_of(source, row):
    y, x, z = row // (X * Z * C), row // (Z * C) % X, row // C % Z
    dy = (source // (X * Z * C) - y) % Y
    dz = (source // C % Z - z) % Z
    second = jnp.where(source % C == 0, dz, dy)
    near = source // (Z * C) % X == x
    return jnp.where(
        near,
        jnp.where(second == 2, 1, 0),
        jnp.where(second == 0, 1, jnp.where(second == 2, 3, 2)),
    )


def work_list(tile_dst, tile_src, live_tiles, row):
    tiles = jnp.arange(tile_src.shape[0], dtype=jnp.int32)
    live = tiles < live_tiles
    phase = phase_of(tile_src // DEV_BLOCKS, row)
    key = jnp.where(live, phase * DSTS + tile_dst, -1)
    ahead = (key[:, None] == key[None, :]) & (tiles[None, :] < tiles[:, None])
    rank = jnp.sum(ahead.astype(jnp.int32), axis=1)
    base = jnp.where(
        phase == 0,
        PHASE_BASE[0],
        jnp.where(phase == 1, PHASE_BASE[1], jnp.where(phase == 2, PHASE_BASE[2], PHASE_BASE[3])),
    )
    place = jnp.where(live, base + rank // 2 * STEP + tile_dst * 2 + rank % 2, -1)
    value = (tiles << SRC_BITS) + tile_src - ZERO_BLOCK
    hit = place[None, :] == jnp.arange(SLOTS, dtype=jnp.int32)[:, None]
    listed = jnp.sum(jnp.where(hit, value[None, :], 0), axis=1) + ZERO_BLOCK
    buckets = jnp.arange(len(PHASE_STEPS) * DSTS, dtype=jnp.int32)
    counts = jnp.sum((key[None, :] == buckets[:, None]).astype(jnp.int32), axis=1)
    steps = jnp.max((counts.reshape(len(PHASE_STEPS), DSTS) + 1) // 2, axis=1)
    return listed, steps


def phase_kernel(phase, counts, spots, first, last, meta, tiles, *refs):
    pieces = refs[: len(counts)]
    refs = refs[len(counts) :]
    if not first:
        before, refs = refs[0], refs[1:]
    near, away, fbuf, ring, acc, fsem, tsem = refs
    steps = meta[SLOTS + 64 + phase]
    half = meta[SLOTS + 64 + 4]
    arrivals = []
    for piece, count, spot in zip(pieces, counts, spots):
        for i in range(count):
            arrivals.append(
                pltpu.make_async_copy(
                    piece.at[pl.ds(i * DEV_BLOCKS, DEV_BLOCKS)],
                    fbuf.at[pl.ds(meta[SLOTS + spot + i] * DEV_BLOCKS, DEV_BLOCKS)],
                    fsem,
                )
            )
    for copy in arrivals:
        copy.start()

    def fetch(step):
        slot = lax.rem(step, RING)
        for i in range(STEP):
            tile = meta[PHASE_BASE[phase] + step * STEP + i] >> SRC_BITS
            pltpu.make_async_copy(tiles.at[tile], ring.at[slot, i], tsem.at[slot]).start()

    def prime(step, carry):
        fetch(step)
        return carry

    lax.fori_loop(0, jnp.minimum(steps, RING), prime, 0)
    fbuf[ZERO_BLOCK] = jnp.zeros(fbuf.shape[1:], fbuf.dtype)
    acc[...] = jnp.zeros_like(acc)
    if not first:
        if last:
            acc[pl.ds(half * DEV_BLOCKS, DEV_BLOCKS)] = before[...]
        else:
            acc[...] = before[...]
    for copy in arrivals:
        copy.wait()

    def run(step, carry):
        slot = lax.rem(step, RING)
        pltpu.make_async_copy(tiles.at[pl.ds(0, STEP)], ring.at[slot], tsem.at[slot]).wait()
        for d in range(DSTS):
            entry = PHASE_BASE[phase] + step * STEP + 2 * d
            blocks = [fbuf[meta[entry + i] & ((1 << SRC_BITS) - 1)] for i in range(2)]
            left = jnp.concatenate([ring[slot, 2 * d], ring[slot, 2 * d + 1]], axis=1)
            acc[d] += jnp.dot(left, jnp.concatenate(blocks, axis=0), preferred_element_type=jnp.float32)

        @pl.when(step + RING < steps)
        def _():
            fetch(step + RING)

        return carry

    lax.fori_loop(0, steps, run, 0)
    if away is not None:
        near[...] = acc[pl.ds(half * DEV_BLOCKS, DEV_BLOCKS)]
        away[...] = acc[pl.ds((1 - half) * DEV_BLOCKS, DEV_BLOCKS)].astype(away.dtype)
    else:
        near[...] = acc[...]


def run_phase(phase, meta, tiles, pieces, counts, spots, before):
    first, last = phase == 0, phase == 3
    whole = (DSTS,) + (128, 256)
    part = (DEV_BLOCKS,) + (128, 256)
    vmem = pl.BlockSpec(memory_space=pltpu.VMEM)
    anyspace = pl.BlockSpec(memory_space=pl.ANY)
    split = phase >= 2
    if split:
        out_shape = (
            jax.ShapeDtypeStruct(part, jnp.float32),
            jax.ShapeDtypeStruct(part, jnp.bfloat16 if last else jnp.float32),
        )
    else:
        out_shape = (jax.ShapeDtypeStruct(whole, jnp.float32),)

    def body(*refs):
        refs = list(refs)
        if not split:
            refs.insert(len(refs) - 5, None)
        phase_kernel(phase, counts, spots, first, last, *refs)

    slots = STEP * PHASE_STEPS[phase]
    return pl.pallas_call(
        body,
        out_shape=out_shape,
        grid_spec=pltpu.PrefetchScalarGridSpec(
            num_scalar_prefetch=1,
            grid=(),
            in_specs=[anyspace] * (1 + len(pieces)) + ([] if first else [vmem]),
            out_specs=(vmem,) * len(out_shape),
            scratch_shapes=[
                pltpu.VMEM((ZERO_BLOCK + 1, 128, 256), jnp.bfloat16),
                pltpu.VMEM((RING, STEP, 128, 128), jnp.bfloat16),
                pltpu.VMEM(whole, jnp.float32),
                pltpu.SemaphoreType.DMA(()),
                pltpu.SemaphoreType.DMA((RING,)),
            ],
        ),
        compiler_params=pltpu.CompilerParams(vmem_limit_bytes=28 << 20),
        cost_estimate=pl.CostEstimate(
            flops=slots * 128 * 128 * 256, bytes_accessed=slots * 8 * 1024, transcendentals=0
        ),
        name="phase",
    )(meta, tiles, *pieces, *(() if first else (before,)))


def on_device(
    features, tile_vals, tile_dst, tile_src, tile_count, degree, w_self, w_neigh, out_bias
):
    row, rep = lax.axis_index("row"), lax.axis_index("rep")
    core = row % C
    phases = own_pieces(features)
    listed, steps = work_list(tile_dst, tile_src, tile_count[0], row)
    table, groups = [], []
    for own in phases:
        pieces, counts, spots = [], [], []
        for sibling in (False, True):
            for rows, places in own:
                spots.append(len(table))
                counts.append(len(places))
                table += owners(places, row, 1 - core if sibling else core)
                rows = send(rows, shift(c=1)) if sibling else rows
                pieces.append(rows.reshape(-1, 128, 256))
        groups.append((pieces, counts, spots))
    meta = jnp.concatenate([listed, jnp.stack(table), steps, rep[None]]).astype(jnp.int32)

    total = None
    for phase, (pieces, counts, spots) in enumerate(groups):
        if phase == 3:
            total, away = total
            early = lax.ppermute(away, "rep", [(0, 1), (1, 0)])
            total, away = run_phase(phase, meta, tile_vals, pieces, counts, spots, total)
            late = lax.ppermute(away, "rep", [(0, 1), (1, 0)])
        else:
            total = run_phase(phase, meta, tile_vals, pieces, counts, spots, total)
            if phase < 2:
                total = total[0]
    summed = (total + early + late.astype(jnp.float32)).reshape(DEV_ROWS, 256)
    neighbours = (summed / jnp.sqrt(degree.astype(jnp.float32))[:, None]).astype(jnp.bfloat16)
    mixed = jnp.dot(features, w_self, preferred_element_type=jnp.float32) + out_bias[None, :]
    mixed = mixed + jnp.dot(neighbours, w_neigh, preferred_element_type=jnp.float32)
    return jnp.maximum(mixed, 0.0).astype(jnp.bfloat16)


def solution(mesh):
    in_specs = (
        P(("rep", "row"), None),
        P(("rep", "row"), None, None),
        P(("rep", "row")),
        P(("rep", "row")),
        P(("rep", "row")),
        P(("rep", "row")),
        P(),
        P(),
        P(),
    )
    out_specs = P(("rep", "row"), None)
    return jax.shard_map(
        on_device, mesh=mesh, in_specs=in_specs, out_specs=out_specs, check_vma=False
    )
```

```python
import functools

import jax
import jax.numpy as jnp
from jax import lax
from jax.experimental import pallas as pl
from jax.experimental.pallas import tpu as pltpu
from jax.sharding import PartitionSpec as P

Y, X, Z, C = 4, 2, 4, 2
DEV_ROWS = 512
DEV_BLOCKS = 4
DSTS = 8
DEPTH = 4
STEP = DEPTH * DSTS
BLOCK_BITS = 9
OWNER_TILES = DEV_BLOCKS * DSTS
CHUNK = 16
GROUP = 8
PHASE_GROUPS = (1, 3, 3, 1)
GROUP_BASE = tuple(sum(PHASE_GROUPS[:i]) for i in range(4))
GROUPS = sum(PHASE_GROUPS)
GROUP_STEPS = GROUP * DEV_BLOCKS // DEPTH
SLOTS = STEP * GROUP_STEPS * GROUPS
OWNERS = GROUP * GROUPS
STARTS, FILLS = SLOTS, SLOTS + OWNERS
STEPS_AT = FILLS + OWNERS
HALF_AT = STEPS_AT + GROUPS
SPLIT = (1, 3)
VMEM_BYTES = 44 << 20
LINE = (0, -1, 1, 2)
HEAD, TAIL = LINE[:2], LINE[2:]


def row_id(y, x, z, c):
    return ((y % Y * X + x % X) * Z + z % Z) * C + c % C


def shift(y=(0, 0), x=0, z=(0, 0), c=0):
    return [
        (row_id(i, j, k, m), row_id(i + y[m], j + x, k + z[m], m + c))
        for i in range(Y) for j in range(X) for k in range(Z) for m in range(C)
    ]


def along_first(step):
    return shift(y=(step, 0), z=(0, step))


def along_second(step):
    return shift(y=(0, step), z=(step, 0))


def send(rows, pairs):
    return lax.ppermute(rows, "row", pairs)


def line_of(plane, second, places=LINE):
    return [(plane, first, second) for first in places]


PLACES = (
    (line_of(0, 0),),
    (line_of(0, -1), line_of(0, 1), line_of(0, 2, HEAD), line_of(0, 2, TAIL)),
    (line_of(1, 0), line_of(1, -1), line_of(1, 1)),
    (line_of(1, 2, HEAD), line_of(1, 2, TAIL)),
)


def owners(places, row, core):
    y, x, z = row // (X * Z * C), row // (Z * C) % X, row // C % Z
    found = []
    for plane, first, second in places:
        dy = jnp.where(core == 0, first, second)
        dz = jnp.where(core == 0, second, first)
        found.append(row_id(y + dy, x + plane, z + dz, core))
    return found


def work_list(tile_dst, tile_src, live_tiles, row):
    core = row % C
    table = []
    for phase in PLACES:
        for holder in (core, 1 - core):
            for places in phase:
                table += owners(places, row, holder)
    table = jnp.stack(table)
    tiles = jnp.arange(tile_src.shape[0], dtype=jnp.int32)
    live = tiles < live_tiles
    owner = tile_src // DEV_BLOCKS
    below = live[None, :] & (owner[None, :] < table[:, None])
    upto = live[None, :] & (owner[None, :] <= table[:, None])
    starts = jnp.minimum(jnp.sum(below.astype(jnp.int32), axis=1), tile_src.shape[0] - OWNER_TILES)
    fills = jnp.sum(upto.astype(jnp.int32), axis=1) - starts
    mine = owner[:, None] == table[None, :]
    spots = jnp.arange(OWNERS, dtype=jnp.int32)
    spot = jnp.sum(jnp.where(mine, spots[None, :], 0), axis=1)
    start = jnp.sum(jnp.where(mine, starts[None, :], 0), axis=1)
    group = spot // GROUP
    first = sum(jnp.where(group >= base, GROUP * (base - last), 0) for last, base in zip(GROUP_BASE, GROUP_BASE[1:]))
    local = spot - first
    key = jnp.where(live, group * DSTS + tile_dst, -1)
    ahead = (key[:, None] == key[None, :]) & (tiles[None, :] < tiles[:, None])
    rank = jnp.sum(ahead.astype(jnp.int32), axis=1)
    step = group * GROUP_STEPS + rank // DEPTH
    place = jnp.where(live, step * STEP + tile_dst * DEPTH + rank % DEPTH, -1)
    held = local * OWNER_TILES + tiles - start
    value = (held << BLOCK_BITS) + 1 + local * DEV_BLOCKS + tile_src % DEV_BLOCKS
    hit = place[None, :] == jnp.arange(SLOTS, dtype=jnp.int32)[:, None]
    listed = jnp.sum(jnp.where(hit, value[None, :], 0), axis=1)
    buckets = jnp.arange(GROUPS * DSTS, dtype=jnp.int32)
    counts = jnp.sum((key[None, :] == buckets[:, None]).astype(jnp.int32), axis=1)
    steps = jnp.max((counts.reshape(GROUPS, DSTS) + DEPTH - 1) // DEPTH, axis=1)
    return listed, starts, fills, steps


def phase_kernel(phase, counts, meta, tiles, *refs):
    pieces = refs[: len(counts)]
    refs = refs[len(counts) :]
    if phase > 0:
        before, refs = refs[0], refs[1:]
    fbuf, tbuf, acc, sem = refs[-4:]
    outs = refs[:-4]
    half = meta[HALF_AT]
    groups = PHASE_GROUPS[phase]
    arrivals = [[] for _ in range(groups)]
    owner = 0
    for piece, count in zip(pieces, counts):
        blocks = fbuf.at[pl.ds(1 + owner * DEV_BLOCKS, count * DEV_BLOCKS)]
        group = owner // GROUP
        arrivals[group].append(pltpu.make_async_copy(piece, blocks, sem.at[group]))
        owner += count

    def tile_copy(i, part):
        start = meta[STARTS + GROUP_BASE[phase] * GROUP + i] + part * CHUNK
        held = tbuf.at[pl.ds(i * OWNER_TILES + part * CHUNK, CHUNK)]
        return pltpu.make_async_copy(tiles.at[pl.ds(start, CHUNK)], held, sem.at[i // GROUP])

    def over(i):
        return meta[FILLS + GROUP_BASE[phase] * GROUP + i] > CHUNK

    for group in range(groups):
        mine = range(group * GROUP, (group + 1) * GROUP)
        arrivals[group] += [tile_copy(i, 0) for i in mine]
        for copy in arrivals[group]:
            copy.start()
        for i in mine:
            pl.when(over(i))(tile_copy(i, 1).start)
    fbuf[0] = jnp.zeros(fbuf.shape[1:], fbuf.dtype)
    if phase == 0:
        acc[...] = jnp.zeros_like(acc)
    elif phase - 1 in SPLIT:
        acc[...] = jnp.zeros_like(acc)
        acc[pl.ds(half * DEV_BLOCKS, DEV_BLOCKS)] = before[...]
    else:
        acc[...] = before[...]

    for group in range(groups):
        for copy in arrivals[group]:
            copy.wait()
        for i in range(group * GROUP, (group + 1) * GROUP):
            pl.when(over(i))(tile_copy(i, 1).wait)
        listed = (GROUP_BASE[phase] + group) * GROUP_STEPS * STEP

        def run(step, carry, listed=listed):
            for d in range(DSTS):
                at = listed + step * STEP + DEPTH * d
                entries = [meta[at + i] for i in range(DEPTH)]
                left = jnp.concatenate([tbuf[e >> BLOCK_BITS] for e in entries], axis=1)
                right = jnp.concatenate([fbuf[e & ((1 << BLOCK_BITS) - 1)] for e in entries], axis=0)
                acc[d] += jnp.dot(left, right, preferred_element_type=jnp.float32)
            return carry

        lax.fori_loop(0, meta[STEPS_AT + GROUP_BASE[phase] + group], run, 0)
    if len(outs) == 2:
        near, away = outs
        near[...] = acc[pl.ds(half * DEV_BLOCKS, DEV_BLOCKS)]
        away[...] = acc[pl.ds((1 - half) * DEV_BLOCKS, DEV_BLOCKS)].astype(away.dtype)
    else:
        outs[0][...] = acc[...]


def run_phase(phase, meta, tiles, pieces, before=None):
    edge, width = tiles.shape[1], pieces[0].shape[1]
    whole, part = (DSTS, edge, width), (DEV_BLOCKS, edge, width)
    vmem = pl.BlockSpec(memory_space=pltpu.VMEM)
    anyspace = pl.BlockSpec(memory_space=pl.ANY)
    f32 = functools.partial(jax.ShapeDtypeStruct, dtype=jnp.float32)
    sent = jnp.float32 if phase == SPLIT[0] else jnp.bfloat16
    out_shape = (f32(part), jax.ShapeDtypeStruct(part, sent)) if phase in SPLIT else (f32(whole),)
    count = GROUP * PHASE_GROUPS[phase]
    blocks = [piece.reshape(-1, edge, width) for piece in pieces]
    counts = [piece.shape[0] // DEV_BLOCKS for piece in blocks]
    slots = STEP * GROUP_STEPS * PHASE_GROUPS[phase] // 2
    results = pl.pallas_call(
        functools.partial(phase_kernel, phase, counts),
        out_shape=out_shape,
        grid_spec=pltpu.PrefetchScalarGridSpec(
            num_scalar_prefetch=1,
            grid=(),
            in_specs=[anyspace] * (1 + len(blocks)) + ([vmem] if phase else []),
            out_specs=(vmem,) * len(out_shape),
            scratch_shapes=[
                pltpu.VMEM((1 + count * DEV_BLOCKS, edge, width), pieces[0].dtype),
                pltpu.VMEM((count * OWNER_TILES, edge, edge), tiles.dtype),
                pltpu.VMEM(whole, jnp.float32),
                pltpu.SemaphoreType.DMA((PHASE_GROUPS[phase],)),
            ],
        ),
        compiler_params=pltpu.CompilerParams(vmem_limit_bytes=VMEM_BYTES),
        cost_estimate=pl.CostEstimate(
            flops=slots * 128 * 128 * 256 * 2, bytes_accessed=slots * 32 * 1024, transcendentals=0
        ),
        name="phase",
    )(meta, tiles, *blocks, *((before,) if phase else ()))
    return results if len(results) > 1 else results[0]


def both(pieces):
    return list(pieces) + [send(rows, shift(c=1)) for rows in pieces]


def on_device(
    features, tile_vals, tile_dst, tile_src, tile_count, degree, w_self, w_neigh, out_bias
):
    row, rep = lax.axis_index("row"), lax.axis_index("rep")
    swap = [(0, 1), (1, 0)]
    hold = lax.optimization_barrier
    from_minus = send(features, along_first(1))
    from_plus = send(features, along_first(-1))
    from_far = send(features, along_first(2))
    across = send(features, shift(x=1))
    listed, starts, fills, steps = work_list(tile_dst, tile_src, tile_count[0], row)
    meta = jnp.concatenate([listed, starts, fills, steps, rep[None]]).astype(jnp.int32)
    from_minus, from_plus, from_far, across, meta = hold((from_minus, from_plus, from_far, across, meta))
    line = jnp.concatenate([features, from_minus, from_plus, from_far])
    rest = send(line[DEV_ROWS:], shift(x=1))
    minus = send(line, along_second(1))
    plus = send(line, along_second(-1))
    total = run_phase(0, meta, tile_vals, both((line,)))
    minus, plus, total = hold((minus, plus, total))
    far_head = send(minus[: 2 * DEV_ROWS], along_second(1))
    far_tail = send(plus[2 * DEV_ROWS :], along_second(-1))
    near_siblings = both((minus, plus))[2:]
    other = jnp.concatenate([across, rest])
    other_minus = send(other, along_second(1))
    other_plus = send(other, along_second(-1))
    far_siblings = both((far_head, far_tail))[2:]

    pieces = [minus, plus, far_head, far_tail] + near_siblings + far_siblings
    near, away = run_phase(1, meta, tile_vals, pieces, total)
    early = lax.ppermute(away, "rep", swap)
    other_minus, other_plus, near = hold((other_minus, other_plus, near))
    last_head = send(other_minus[: 2 * DEV_ROWS], along_second(1))
    last_tail = send(other_plus[2 * DEV_ROWS :], along_second(-1))

    total = run_phase(2, meta, tile_vals, both((other, other_minus, other_plus)), near)
    last_head, last_tail, total, early = hold((last_head, last_tail, total, early))
    near, away = run_phase(3, meta, tile_vals, both((last_head, last_tail)), total)
    late = lax.ppermute(away, "rep", swap)
    summed = (near + early + late.astype(jnp.float32)).reshape(features.shape)
    neighbours = (summed / jnp.sqrt(degree.astype(jnp.float32))[:, None]).astype(jnp.bfloat16)
    mixed = jnp.dot(features, w_self, preferred_element_type=jnp.float32) + out_bias[None, :]
    mixed = mixed + jnp.dot(neighbours, w_neigh, preferred_element_type=jnp.float32)
    return jnp.maximum(mixed, 0.0).astype(jnp.bfloat16)


def solution(mesh):
    in_specs = (
        P(("rep", "row"), None),
        P(("rep", "row"), None, None),
        P(("rep", "row")),
        P(("rep", "row")),
        P(("rep", "row")),
        P(("rep", "row")),
        P(),
        P(),
        P(),
    )
    out_specs = P(("rep", "row"), None)
    return jax.shard_map(
        on_device, mesh=mesh, in_specs=in_specs, out_specs=out_specs, check_vma=False
    )
```

```python
import functools

import jax
import jax.numpy as jnp
from jax import lax
from jax.experimental import pallas as pl
from jax.experimental.pallas import tpu as pltpu
from jax.sharding import PartitionSpec as P

Y, X, Z, C = 4, 2, 4, 2
DEV_ROWS = 512
DEV_BLOCKS = 4
DSTS = 8
DEPTH = 4
STEP = DEPTH * DSTS
BLOCK_BITS = 9
OWNER_TILES = DEV_BLOCKS * DSTS
CHUNK = 16
GROUP = 8
PHASE_GROUPS = (1, 3, 3, 1)
GROUP_BASE = tuple(sum(PHASE_GROUPS[:i]) for i in range(4))
GROUPS = sum(PHASE_GROUPS)
GROUP_STEPS = GROUP * DEV_BLOCKS // DEPTH
SLOTS = STEP * GROUP_STEPS * GROUPS
OWNERS = GROUP * GROUPS
STARTS, FILLS = SLOTS, SLOTS + OWNERS
STEPS_AT = FILLS + OWNERS
HALF_AT = STEPS_AT + GROUPS
SPLIT = (1, 3)
VMEM_BYTES = 44 << 20
LINE = (0, -1, 1, 2)
HEAD, TAIL = LINE[:2], LINE[2:]


def row_id(y, x, z, c):
    return ((y % Y * X + x % X) * Z + z % Z) * C + c % C


def shift(y=(0, 0), x=0, z=(0, 0), c=0):
    return [
        (row_id(i, j, k, m), row_id(i + y[m], j + x, k + z[m], m + c))
        for i in range(Y) for j in range(X) for k in range(Z) for m in range(C)
    ]


def along_first(step):
    return shift(y=(step, 0), z=(0, step))


def along_second(step):
    return shift(y=(0, step), z=(step, 0))


def send(rows, pairs):
    return lax.ppermute(rows, "row", pairs)


def line_of(plane, second, places=LINE):
    return [(plane, first, second) for first in places]


PLACES = (
    (line_of(0, 0),),
    (line_of(0, -1), line_of(0, 1), line_of(0, 2, HEAD), line_of(0, 2, TAIL)),
    (line_of(1, 0), line_of(1, -1), line_of(1, 1)),
    (line_of(1, 2, HEAD), line_of(1, 2, TAIL)),
)


def owners(places, row, core):
    y, x, z = row // (X * Z * C), row // (Z * C) % X, row // C % Z
    found = []
    for plane, first, second in places:
        dy = jnp.where(core == 0, first, second)
        dz = jnp.where(core == 0, second, first)
        found.append(row_id(y + dy, x + plane, z + dz, core))
    return found


def work_list(tile_dst, tile_src, live_tiles, row):
    core = row % C
    table = []
    for phase in PLACES:
        for holder in (core, 1 - core):
            for places in phase:
                table += owners(places, row, holder)
    table = jnp.stack(table)
    tiles = jnp.arange(tile_src.shape[0], dtype=jnp.int32)
    live = tiles < live_tiles
    owner = tile_src // DEV_BLOCKS
    below = live[None, :] & (owner[None, :] < table[:, None])
    upto = live[None, :] & (owner[None, :] <= table[:, None])
    starts = jnp.minimum(jnp.sum(below.astype(jnp.int32), axis=1), tile_src.shape[0] - OWNER_TILES)
    fills = jnp.sum(upto.astype(jnp.int32), axis=1) - starts
    mine = owner[:, None] == table[None, :]
    spots = jnp.arange(OWNERS, dtype=jnp.int32)
    spot = jnp.sum(jnp.where(mine, spots[None, :], 0), axis=1)
    start = jnp.sum(jnp.where(mine, starts[None, :], 0), axis=1)
    group = spot // GROUP
    first = sum(jnp.where(group >= base, GROUP * (base - last), 0) for last, base in zip(GROUP_BASE, GROUP_BASE[1:]))
    local = spot - first
    key = jnp.where(live, group * DSTS + tile_dst, -1)
    ahead = (key[:, None] == key[None, :]) & (tiles[None, :] < tiles[:, None])
    rank = jnp.sum(ahead.astype(jnp.int32), axis=1)
    step = group * GROUP_STEPS + rank // DEPTH
    place = jnp.where(live, step * STEP + tile_dst * DEPTH + rank % DEPTH, -1)
    held = local * OWNER_TILES + tiles - start
    value = (held << BLOCK_BITS) + 1 + local * DEV_BLOCKS + tile_src % DEV_BLOCKS
    hit = place[None, :] == jnp.arange(SLOTS, dtype=jnp.int32)[:, None]
    listed = jnp.sum(jnp.where(hit, value[None, :], 0), axis=1)
    buckets = jnp.arange(GROUPS * DSTS, dtype=jnp.int32)
    counts = jnp.sum((key[None, :] == buckets[:, None]).astype(jnp.int32), axis=1)
    steps = jnp.max((counts.reshape(GROUPS, DSTS) + DEPTH - 1) // DEPTH, axis=1)
    return listed, starts, fills, steps


def phase_kernel(phase, counts, meta, tiles, *refs):
    pieces = refs[: len(counts)]
    refs = refs[len(counts) :]
    if phase > 0:
        before, refs = refs[0], refs[1:]
    fbuf, tbuf, acc, sem = refs[-4:]
    outs = refs[:-4]
    half = meta[HALF_AT]
    groups = PHASE_GROUPS[phase]
    arrivals = [[] for _ in range(groups)]
    owner = 0
    for piece, count in zip(pieces, counts):
        blocks = fbuf.at[pl.ds(1 + owner * DEV_BLOCKS, count * DEV_BLOCKS)]
        group = owner // GROUP
        arrivals[group].append(pltpu.make_async_copy(piece, blocks, sem.at[group]))
        owner += count

    def tile_copy(i, part):
        start = meta[STARTS + GROUP_BASE[phase] * GROUP + i] + part * CHUNK
        held = tbuf.at[pl.ds(i * OWNER_TILES + part * CHUNK, CHUNK)]
        return pltpu.make_async_copy(tiles.at[pl.ds(start, CHUNK)], held, sem.at[i // GROUP])

    def over(i):
        return meta[FILLS + GROUP_BASE[phase] * GROUP + i] > CHUNK

    for group in range(groups):
        mine = range(group * GROUP, (group + 1) * GROUP)
        arrivals[group] += [tile_copy(i, 0) for i in mine]
        for copy in arrivals[group]:
            copy.start()
        for i in mine:
            pl.when(over(i))(tile_copy(i, 1).start)
    fbuf[0] = jnp.zeros(fbuf.shape[1:], fbuf.dtype)
    if phase == 0:
        acc[...] = jnp.zeros_like(acc)
    elif phase - 1 in SPLIT:
        acc[...] = jnp.zeros_like(acc)
        acc[pl.ds(half * DEV_BLOCKS, DEV_BLOCKS)] = before[...]
    else:
        acc[...] = before[...]

    for group in range(groups):
        for copy in arrivals[group]:
            copy.wait()
        for i in range(group * GROUP, (group + 1) * GROUP):
            pl.when(over(i))(tile_copy(i, 1).wait)
        listed = (GROUP_BASE[phase] + group) * GROUP_STEPS * STEP

        def run(step, carry, listed=listed):
            for d in range(DSTS):
                at = listed + step * STEP + DEPTH * d
                entries = [meta[at + i] for i in range(DEPTH)]
                left = jnp.concatenate([tbuf[e >> BLOCK_BITS] for e in entries], axis=1)
                right = jnp.concatenate([fbuf[e & ((1 << BLOCK_BITS) - 1)] for e in entries], axis=0)
                acc[d] += jnp.dot(left, right, preferred_element_type=jnp.float32)
            return carry

        lax.fori_loop(0, meta[STEPS_AT + GROUP_BASE[phase] + group], run, 0)
    if len(outs) == 2:
        near, away = outs
        near[...] = acc[pl.ds(half * DEV_BLOCKS, DEV_BLOCKS)]
        away[...] = acc[pl.ds((1 - half) * DEV_BLOCKS, DEV_BLOCKS)].astype(away.dtype)
    else:
        outs[0][...] = acc[...]


def run_phase(phase, meta, tiles, pieces, before=None):
    edge, width = tiles.shape[1], pieces[0].shape[1]
    whole, part = (DSTS, edge, width), (DEV_BLOCKS, edge, width)
    vmem = pl.BlockSpec(memory_space=pltpu.VMEM)
    anyspace = pl.BlockSpec(memory_space=pl.ANY)
    f32 = functools.partial(jax.ShapeDtypeStruct, dtype=jnp.float32)
    sent = jnp.float32 if phase == SPLIT[0] else jnp.bfloat16
    out_shape = (f32(part), jax.ShapeDtypeStruct(part, sent)) if phase in SPLIT else (f32(whole),)
    count = GROUP * PHASE_GROUPS[phase]
    blocks = [piece.reshape(-1, edge, width) for piece in pieces]
    counts = [piece.shape[0] // DEV_BLOCKS for piece in blocks]
    slots = STEP * GROUP_STEPS * PHASE_GROUPS[phase] // 2
    results = pl.pallas_call(
        functools.partial(phase_kernel, phase, counts),
        out_shape=out_shape,
        grid_spec=pltpu.PrefetchScalarGridSpec(
            num_scalar_prefetch=1,
            grid=(),
            in_specs=[anyspace] * (1 + len(blocks)) + ([vmem] if phase else []),
            out_specs=(vmem,) * len(out_shape),
            scratch_shapes=[
                pltpu.VMEM((1 + count * DEV_BLOCKS, edge, width), pieces[0].dtype),
                pltpu.VMEM((count * OWNER_TILES, edge, edge), tiles.dtype),
                pltpu.VMEM(whole, jnp.float32),
                pltpu.SemaphoreType.DMA((PHASE_GROUPS[phase],)),
            ],
        ),
        compiler_params=pltpu.CompilerParams(vmem_limit_bytes=VMEM_BYTES),
        cost_estimate=pl.CostEstimate(
            flops=slots * 128 * 128 * 256 * 2, bytes_accessed=slots * 32 * 1024, transcendentals=0
        ),
        name="phase",
    )(meta, tiles, *blocks, *((before,) if phase else ()))
    return results if len(results) > 1 else results[0]


def both(pieces):
    return list(pieces) + [send(rows, shift(c=1)) for rows in pieces]


def on_device(
    features, tile_vals, tile_dst, tile_src, tile_count, degree, w_self, w_neigh, out_bias
):
    row, rep = lax.axis_index("row"), lax.axis_index("rep")
    swap = [(0, 1), (1, 0)]
    hold = lax.optimization_barrier
    from_minus = send(features, along_first(1))
    from_plus = send(features, along_first(-1))
    from_far = send(features, along_first(2))
    across = send(features, shift(x=1))
    listed, starts, fills, steps = work_list(tile_dst, tile_src, tile_count[0], row)
    meta = jnp.concatenate([listed, starts, fills, steps, rep[None]]).astype(jnp.int32)
    from_minus, from_plus, from_far, across, meta = hold((from_minus, from_plus, from_far, across, meta))
    line = jnp.concatenate([features, from_minus, from_plus, from_far])
    rest = send(line[DEV_ROWS:], shift(x=1))
    minus = send(line, along_second(1))
    plus = send(line, along_second(-1))
    total = run_phase(0, meta, tile_vals, both((line,)))
    minus, plus, total = hold((minus, plus, total))
    far_head = send(minus[: 2 * DEV_ROWS], along_second(1))
    far_tail = send(plus[2 * DEV_ROWS :], along_second(-1))
    near_siblings = both((minus, plus))[2:]
    other = jnp.concatenate([across, rest])
    other_minus = send(other, along_second(1))
    other_plus = send(other, along_second(-1))
    far_siblings = both((far_head, far_tail))[2:]

    pieces = [minus, plus, far_head, far_tail] + near_siblings + far_siblings
    near, away = run_phase(1, meta, tile_vals, pieces, total)
    early = lax.ppermute(away, "rep", swap)
    other_minus, other_plus, near = hold((other_minus, other_plus, near))
    last_head = send(other_minus[: 2 * DEV_ROWS], along_second(1))
    last_tail = send(other_plus[2 * DEV_ROWS :], along_second(-1))

    total = run_phase(2, meta, tile_vals, both((other, other_minus, other_plus)), near)
    last_head, last_tail, total = hold((last_head, last_tail, total))
    last = both((last_head, last_tail))
    total, early = hold((total, early))
    near, away = run_phase(3, meta, tile_vals, last, total)
    late = lax.ppermute(away, "rep", swap)
    summed = (near + early + late.astype(jnp.float32)).reshape(features.shape)
    neighbours = (summed / jnp.sqrt(degree.astype(jnp.float32))[:, None]).astype(jnp.bfloat16)
    mixed = jnp.dot(features, w_self, preferred_element_type=jnp.float32) + out_bias[None, :]
    mixed = mixed + jnp.dot(neighbours, w_neigh, preferred_element_type=jnp.float32)
    return jnp.maximum(mixed, 0.0).astype(jnp.bfloat16)


def solution(mesh):
    in_specs = (
        P(("rep", "row"), None),
        P(("rep", "row"), None, None),
        P(("rep", "row")),
        P(("rep", "row")),
        P(("rep", "row")),
        P(("rep", "row")),
        P(),
        P(),
        P(),
    )
    out_specs = P(("rep", "row"), None)
    return jax.shard_map(
        on_device, mesh=mesh, in_specs=in_specs, out_specs=out_specs, check_vma=False
    )
```

```python
import functools

import jax
import jax.numpy as jnp
from jax import lax
from jax.experimental import pallas as pl
from jax.experimental.pallas import tpu as pltpu
from jax.sharding import PartitionSpec as P

Y, X, Z, C = 4, 2, 4, 2
DEV_ROWS = 512
DEV_BLOCKS = 4
DSTS = 8
DEPTH = 4
STEP = DEPTH * DSTS
BLOCK_BITS = 9
OWNER_TILES = DEV_BLOCKS * DSTS
CHUNK = 16
GROUP = 8
PHASE_GROUPS = (1, 3, 3, 1)
GROUP_BASE = tuple(sum(PHASE_GROUPS[:i]) for i in range(4))
GROUPS = sum(PHASE_GROUPS)
GROUP_STEPS = GROUP * DEV_BLOCKS // DEPTH
SLOTS = STEP * GROUP_STEPS * GROUPS
OWNERS = GROUP * GROUPS
SPLIT = (1, 3)
VMEM_BYTES = 44 << 20
LINE = (0, -1, 1, 2)
HEAD, TAIL = LINE[:2], LINE[2:]


def row_id(y, x, z, c):
    return ((y % Y * X + x % X) * Z + z % Z) * C + c % C


def shift(y=(0, 0), x=0, z=(0, 0), c=0):
    return [
        (row_id(i, j, k, m), row_id(i + y[m], j + x, k + z[m], m + c))
        for i in range(Y) for j in range(X) for k in range(Z) for m in range(C)
    ]


def along_first(step):
    return shift(y=(step, 0), z=(0, step))


def along_second(step):
    return shift(y=(0, step), z=(step, 0))


def send(rows, pairs):
    return lax.ppermute(rows, "row", pairs)


def line_of(plane, second, places=LINE):
    return [(plane, first, second) for first in places]


PLACES = (
    (line_of(0, 0),),
    (line_of(0, -1), line_of(0, 1), line_of(0, 2, HEAD), line_of(0, 2, TAIL)),
    (line_of(1, 0), line_of(1, -1), line_of(1, 1)),
    (line_of(1, 2, HEAD), line_of(1, 2, TAIL)),
)


def owners(places, row, core):
    y, x, z = row // (X * Z * C), row // (Z * C) % X, row // C % Z
    found = []
    for plane, first, second in places:
        dy = jnp.where(core == 0, first, second)
        dz = jnp.where(core == 0, second, first)
        found.append(row_id(y + dy, x + plane, z + dz, core))
    return found


def work_list(tile_dst, tile_src, live_tiles, row):
    core = row % C
    table = []
    for phase in PLACES:
        for holder in (core, 1 - core):
            for places in phase:
                table += owners(places, row, holder)
    table = jnp.stack(table)
    tiles = jnp.arange(tile_src.shape[0], dtype=jnp.int32)
    live = tiles < live_tiles
    owner = tile_src // DEV_BLOCKS
    below = live[None, :] & (owner[None, :] < table[:, None])
    upto = live[None, :] & (owner[None, :] <= table[:, None])
    starts = jnp.minimum(jnp.sum(below.astype(jnp.int32), axis=1), tile_src.shape[0] - OWNER_TILES)
    fills = jnp.sum(upto.astype(jnp.int32), axis=1) - starts
    mine = owner[:, None] == table[None, :]
    spots = jnp.arange(OWNERS, dtype=jnp.int32)
    spot = jnp.sum(jnp.where(mine, spots[None, :], 0), axis=1)
    start = jnp.sum(jnp.where(mine, starts[None, :], 0), axis=1)
    group = spot // GROUP
    first = sum(jnp.where(group >= base, GROUP * (base - last), 0) for last, base in zip(GROUP_BASE, GROUP_BASE[1:]))
    local = spot - first
    key = jnp.where(live, group * DSTS + tile_dst, -1)
    ahead = (key[:, None] == key[None, :]) & (tiles[None, :] < tiles[:, None])
    rank = jnp.sum(ahead.astype(jnp.int32), axis=1)
    step = group * GROUP_STEPS + rank // DEPTH
    place = jnp.where(live, step * STEP + tile_dst * DEPTH + rank % DEPTH, -1)
    held = local * OWNER_TILES + tiles - start
    value = (held << BLOCK_BITS) + 1 + local * DEV_BLOCKS + tile_src % DEV_BLOCKS
    hit = place[None, :] == jnp.arange(SLOTS, dtype=jnp.int32)[:, None]
    listed = jnp.sum(jnp.where(hit, value[None, :], 0), axis=1)
    buckets = jnp.arange(GROUPS * DSTS, dtype=jnp.int32)
    counts = jnp.sum((key[None, :] == buckets[:, None]).astype(jnp.int32), axis=1)
    steps = jnp.max((counts.reshape(GROUPS, DSTS) + DEPTH - 1) // DEPTH, axis=1)
    return listed, starts, fills, steps


def phase_kernel(phase, counts, meta, tiles, *refs):
    pieces = refs[: len(counts)]
    refs = refs[len(counts) :]
    if phase > 0:
        before, refs = refs[0], refs[1:]
    fbuf, tbuf, acc, sem = refs[-4:]
    outs = refs[:-4]
    groups = PHASE_GROUPS[phase]
    starts_at = groups * GROUP_STEPS * STEP
    fills_at = starts_at + groups * GROUP
    steps_at = fills_at + groups * GROUP
    half = meta[steps_at + groups]
    arrivals = [[] for _ in range(groups)]
    owner = 0
    for piece, count in zip(pieces, counts):
        blocks = fbuf.at[pl.ds(1 + owner * DEV_BLOCKS, count * DEV_BLOCKS)]
        group = owner // GROUP
        arrivals[group].append(pltpu.make_async_copy(piece, blocks, sem.at[group]))
        owner += count

    def tile_copy(i, part):
        start = meta[starts_at + i] + part * CHUNK
        held = tbuf.at[pl.ds(i * OWNER_TILES + part * CHUNK, CHUNK)]
        return pltpu.make_async_copy(tiles.at[pl.ds(start, CHUNK)], held, sem.at[i // GROUP])

    def over(i):
        return meta[fills_at + i] > CHUNK

    for group in range(groups):
        mine = range(group * GROUP, (group + 1) * GROUP)
        arrivals[group] += [tile_copy(i, 0) for i in mine]
        for copy in arrivals[group]:
            copy.start()
        for i in mine:
            pl.when(over(i))(tile_copy(i, 1).start)
    fbuf[0] = jnp.zeros(fbuf.shape[1:], fbuf.dtype)
    if phase == 0:
        acc[...] = jnp.zeros_like(acc)
    elif phase - 1 in SPLIT:
        acc[...] = jnp.zeros_like(acc)
        acc[pl.ds(half * DEV_BLOCKS, DEV_BLOCKS)] = before[...]
    else:
        acc[...] = before[...]

    for group in range(groups):
        for copy in arrivals[group]:
            copy.wait()
        for i in range(group * GROUP, (group + 1) * GROUP):
            pl.when(over(i))(tile_copy(i, 1).wait)
        listed = group * GROUP_STEPS * STEP

        def run(step, carry, listed=listed):
            for d in range(DSTS):
                at = listed + step * STEP + DEPTH * d
                entries = [meta[at + i] for i in range(DEPTH)]
                left = jnp.concatenate([tbuf[e >> BLOCK_BITS] for e in entries], axis=1)
                right = jnp.concatenate([fbuf[e & ((1 << BLOCK_BITS) - 1)] for e in entries], axis=0)
                acc[d] += jnp.dot(left, right, preferred_element_type=jnp.float32)
            return carry

        lax.fori_loop(0, meta[steps_at + group], run, 0)
    if len(outs) == 2:
        near, away = outs
        near[...] = acc[pl.ds(half * DEV_BLOCKS, DEV_BLOCKS)]
        away[...] = acc[pl.ds((1 - half) * DEV_BLOCKS, DEV_BLOCKS)].astype(away.dtype)
    else:
        outs[0][...] = acc[...]


def run_phase(phase, meta, tiles, pieces, before=None):
    edge, width = tiles.shape[1], pieces[0].shape[1]
    whole, part = (DSTS, edge, width), (DEV_BLOCKS, edge, width)
    vmem = pl.BlockSpec(memory_space=pltpu.VMEM)
    anyspace = pl.BlockSpec(memory_space=pl.ANY)
    f32 = functools.partial(jax.ShapeDtypeStruct, dtype=jnp.float32)
    sent = jnp.float32 if phase == SPLIT[0] else jnp.bfloat16
    out_shape = (f32(part), jax.ShapeDtypeStruct(part, sent)) if phase in SPLIT else (f32(whole),)
    count = GROUP * PHASE_GROUPS[phase]
    blocks = [piece.reshape(-1, edge, width) for piece in pieces]
    counts = [piece.shape[0] // DEV_BLOCKS for piece in blocks]
    slots = STEP * GROUP_STEPS * PHASE_GROUPS[phase] // 2
    results = pl.pallas_call(
        functools.partial(phase_kernel, phase, counts),
        out_shape=out_shape,
        grid_spec=pltpu.PrefetchScalarGridSpec(
            num_scalar_prefetch=1,
            grid=(),
            in_specs=[anyspace] * (1 + len(blocks)) + ([vmem] if phase else []),
            out_specs=(vmem,) * len(out_shape),
            scratch_shapes=[
                pltpu.VMEM((1 + count * DEV_BLOCKS, edge, width), pieces[0].dtype),
                pltpu.VMEM((count * OWNER_TILES, edge, edge), tiles.dtype),
                pltpu.VMEM(whole, jnp.float32),
                pltpu.SemaphoreType.DMA((PHASE_GROUPS[phase],)),
            ],
        ),
        compiler_params=pltpu.CompilerParams(vmem_limit_bytes=VMEM_BYTES),
        cost_estimate=pl.CostEstimate(
            flops=slots * 128 * 128 * 256 * 2, bytes_accessed=slots * 32 * 1024, transcendentals=0
        ),
        name="phase",
    )(meta, tiles, *blocks, *((before,) if phase else ()))
    return results if len(results) > 1 else results[0]


def both(pieces):
    return list(pieces) + [send(rows, shift(c=1)) for rows in pieces]


def on_device(
    features, tile_vals, tile_dst, tile_src, tile_count, degree, w_self, w_neigh, out_bias
):
    row, rep = lax.axis_index("row"), lax.axis_index("rep")
    swap = [(0, 1), (1, 0)]
    hold = lax.optimization_barrier
    from_minus = send(features, along_first(1))
    from_plus = send(features, along_first(-1))
    from_far = send(features, along_first(2))
    across = send(features, shift(x=1))
    listed, starts, fills, steps = work_list(tile_dst, tile_src, tile_count[0], row)
    meta = []
    for base, groups in zip(GROUP_BASE, PHASE_GROUPS):
        parts = [
            lax.slice_in_dim(values, base * size, (base + groups) * size)
            for values, size in ((listed, GROUP_STEPS * STEP), (starts, GROUP), (fills, GROUP), (steps, 1))
        ]
        meta.append(jnp.concatenate(parts + [rep[None]]).astype(jnp.int32))
    from_minus, from_plus, from_far, across, meta = hold((from_minus, from_plus, from_far, across, meta))
    line = jnp.concatenate([features, from_minus, from_plus, from_far])
    rest = send(line[DEV_ROWS:], shift(x=1))
    minus = send(line, along_second(1))
    plus = send(line, along_second(-1))
    total = run_phase(0, meta[0], tile_vals, both((line,)))
    minus, plus, total = hold((minus, plus, total))
    far_head = send(minus[: 2 * DEV_ROWS], along_second(1))
    far_tail = send(plus[2 * DEV_ROWS :], along_second(-1))
    near_siblings = both((minus, plus))[2:]
    other = jnp.concatenate([across, rest])
    other_minus = send(other, along_second(1))
    other_plus = send(other, along_second(-1))
    far_siblings = both((far_head, far_tail))[2:]

    pieces = [minus, plus, far_head, far_tail] + near_siblings + far_siblings
    near, away = run_phase(1, meta[1], tile_vals, pieces, total)
    early = lax.ppermute(away, "rep", swap)
    other_minus, other_plus, near = hold((other_minus, other_plus, near))
    last_head = send(other_minus[: 2 * DEV_ROWS], along_second(1))
    last_tail = send(other_plus[2 * DEV_ROWS :], along_second(-1))

    total = run_phase(2, meta[2], tile_vals, both((other, other_minus, other_plus)), near)
    last_head, last_tail, total = hold((last_head, last_tail, total))
    last = both((last_head, last_tail))
    total, early = hold((total, early))
    near, away = run_phase(3, meta[3], tile_vals, last, total)
    late = lax.ppermute(away, "rep", swap)
    summed = (near + early + late.astype(jnp.float32)).reshape(features.shape)
    neighbours = (summed / jnp.sqrt(degree.astype(jnp.float32))[:, None]).astype(jnp.bfloat16)
    mixed = jnp.dot(features, w_self, preferred_element_type=jnp.float32) + out_bias[None, :]
    mixed = mixed + jnp.dot(neighbours, w_neigh, preferred_element_type=jnp.float32)
    return jnp.maximum(mixed, 0.0).astype(jnp.bfloat16)


def solution(mesh):
    in_specs = (
        P(("rep", "row"), None),
        P(("rep", "row"), None, None),
        P(("rep", "row")),
        P(("rep", "row")),
        P(("rep", "row")),
        P(("rep", "row")),
        P(),
        P(),
        P(),
    )
    out_specs = P(("rep", "row"), None)
    return jax.shard_map(
        on_device, mesh=mesh, in_specs=in_specs, out_specs=out_specs, check_vma=False
    )
```

```python
import functools

import jax
import jax.numpy as jnp
from jax import lax
from jax.experimental import pallas as pl
from jax.experimental.pallas import tpu as pltpu
from jax.sharding import PartitionSpec as P

Y, X, Z, C = 4, 2, 4, 2
DEV_ROWS = 512
DEV_BLOCKS = 4
DSTS = 8
DEPTH = 4
STEP = DEPTH * DSTS
BLOCK_BITS = 9
OWNER_TILES = DEV_BLOCKS * DSTS
CHUNK = 16
GROUP = 8
PHASE_GROUPS = (1, 3, 3, 1)
GROUP_BASE = tuple(sum(PHASE_GROUPS[:i]) for i in range(4))
GROUPS = sum(PHASE_GROUPS)
GROUP_STEPS = GROUP * DEV_BLOCKS // DEPTH
SLOTS = STEP * GROUP_STEPS * GROUPS
OWNERS = GROUP * GROUPS
SPLIT = (1, 3)
VMEM_BYTES = 39 << 20
LINE = (0, -1, 1, 2)
HEAD, TAIL = LINE[:2], LINE[2:]


def row_id(y, x, z, c):
    return ((y % Y * X + x % X) * Z + z % Z) * C + c % C


def shift(y=(0, 0), x=0, z=(0, 0), c=0):
    return [
        (row_id(i, j, k, m), row_id(i + y[m], j + x, k + z[m], m + c))
        for i in range(Y) for j in range(X) for k in range(Z) for m in range(C)
    ]


def along_first(step):
    return shift(y=(step, 0), z=(0, step))


def along_second(step):
    return shift(y=(0, step), z=(step, 0))


def send(rows, pairs):
    return lax.ppermute(rows, "row", pairs)


def line_of(plane, second, places=LINE):
    return [(plane, first, second) for first in places]


PLACES = (
    (line_of(0, 0),),
    (line_of(0, -1), line_of(0, 1), line_of(0, 2, HEAD), line_of(0, 2, TAIL)),
    (line_of(1, 0), line_of(1, -1), line_of(1, 1)),
    (line_of(1, 2, HEAD), line_of(1, 2, TAIL)),
)


def owners(places, row, core):
    y, x, z = row // (X * Z * C), row // (Z * C) % X, row // C % Z
    found = []
    for plane, first, second in places:
        dy = jnp.where(core == 0, first, second)
        dz = jnp.where(core == 0, second, first)
        found.append(row_id(y + dy, x + plane, z + dz, core))
    return found


def work_list(tile_dst, tile_src, live_tiles, row):
    core = row % C
    table = []
    for phase in PLACES:
        for holder in (core, 1 - core):
            for places in phase:
                table += owners(places, row, holder)
    table = jnp.stack(table)
    tiles = jnp.arange(tile_src.shape[0], dtype=jnp.int32)
    live = tiles < live_tiles
    owner = tile_src // DEV_BLOCKS
    below = live[None, :] & (owner[None, :] < table[:, None])
    upto = live[None, :] & (owner[None, :] <= table[:, None])
    starts = jnp.minimum(jnp.sum(below.astype(jnp.int32), axis=1), tile_src.shape[0] - OWNER_TILES)
    fills = jnp.sum(upto.astype(jnp.int32), axis=1) - starts
    mine = owner[:, None] == table[None, :]
    spots = jnp.arange(OWNERS, dtype=jnp.int32)
    spot = jnp.sum(jnp.where(mine, spots[None, :], 0), axis=1)
    start = jnp.sum(jnp.where(mine, starts[None, :], 0), axis=1)
    group = spot // GROUP
    first = sum(jnp.where(group >= base, GROUP * (base - last), 0) for last, base in zip(GROUP_BASE, GROUP_BASE[1:]))
    local = spot - first
    key = jnp.where(live, group * DSTS + tile_dst, -1)
    ahead = (key[:, None] == key[None, :]) & (tiles[None, :] < tiles[:, None])
    rank = jnp.sum(ahead.astype(jnp.int32), axis=1)
    step = group * GROUP_STEPS + rank // DEPTH
    place = jnp.where(live, step * STEP + tile_dst * DEPTH + rank % DEPTH, -1)
    held = local * OWNER_TILES + tiles - start
    value = (held << BLOCK_BITS) + 1 + local * DEV_BLOCKS + tile_src % DEV_BLOCKS
    hit = place[None, :] == jnp.arange(SLOTS, dtype=jnp.int32)[:, None]
    listed = jnp.sum(jnp.where(hit, value[None, :], 0), axis=1)
    buckets = jnp.arange(GROUPS * DSTS, dtype=jnp.int32)
    counts = jnp.sum((key[None, :] == buckets[:, None]).astype(jnp.int32), axis=1)
    steps = jnp.max((counts.reshape(GROUPS, DSTS) + DEPTH - 1) // DEPTH, axis=1)
    return listed, starts, fills, steps


def phase_kernel(phase, counts, meta, tiles, *refs):
    pieces = refs[: len(counts)]
    refs = refs[len(counts) :]
    if phase > 0:
        before, refs = refs[0], refs[1:]
    fbuf, tbuf, acc, sem = refs[-4:]
    outs = refs[:-4]
    groups = PHASE_GROUPS[phase]
    starts_at = groups * GROUP_STEPS * STEP
    fills_at = starts_at + groups * GROUP
    steps_at = fills_at + groups * GROUP
    half = meta[steps_at + groups]
    arrivals = [[] for _ in range(groups)]
    owner = 0
    for piece, count in zip(pieces, counts):
        blocks = fbuf.at[pl.ds(1 + owner * DEV_BLOCKS, count * DEV_BLOCKS)]
        group = owner // GROUP
        arrivals[group].append(pltpu.make_async_copy(piece, blocks, sem.at[group]))
        owner += count

    def tile_copy(i, part):
        start = meta[starts_at + i] + part * CHUNK
        held = tbuf.at[pl.ds(i * OWNER_TILES + part * CHUNK, CHUNK)]
        return pltpu.make_async_copy(tiles.at[pl.ds(start, CHUNK)], held, sem.at[i // GROUP])

    def over(i):
        return meta[fills_at + i] > CHUNK

    for group in range(groups):
        mine = range(group * GROUP, (group + 1) * GROUP)
        arrivals[group] += [tile_copy(i, 0) for i in mine]
        for copy in arrivals[group]:
            copy.start()
        for i in mine:
            pl.when(over(i))(tile_copy(i, 1).start)
    fbuf[0] = jnp.zeros(fbuf.shape[1:], fbuf.dtype)
    if phase == 0:
        acc[...] = jnp.zeros_like(acc)
    elif phase - 1 in SPLIT:
        acc[...] = jnp.zeros_like(acc)
        acc[pl.ds(half * DEV_BLOCKS, DEV_BLOCKS)] = before[...]
    else:
        acc[...] = before[...]

    for group in range(groups):
        for copy in arrivals[group]:
            copy.wait()
        for i in range(group * GROUP, (group + 1) * GROUP):
            pl.when(over(i))(tile_copy(i, 1).wait)
        listed = group * GROUP_STEPS * STEP

        def run(step, carry, listed=listed):
            for d in range(DSTS):
                at = listed + step * STEP + DEPTH * d
                entries = [meta[at + i] for i in range(DEPTH)]
                left = jnp.concatenate([tbuf[e >> BLOCK_BITS] for e in entries], axis=1)
                right = jnp.concatenate([fbuf[e & ((1 << BLOCK_BITS) - 1)] for e in entries], axis=0)
                acc[d] += jnp.dot(left, right, preferred_element_type=jnp.float32)
            return carry

        lax.fori_loop(0, meta[steps_at + group], run, 0)
    if len(outs) == 2:
        near, away = outs
        near[...] = acc[pl.ds(half * DEV_BLOCKS, DEV_BLOCKS)]
        away[...] = acc[pl.ds((1 - half) * DEV_BLOCKS, DEV_BLOCKS)].astype(away.dtype)
    else:
        outs[0][...] = acc[...]


def run_phase(phase, meta, tiles, pieces, before=None):
    edge, width = tiles.shape[1], pieces[0].shape[1]
    whole, part = (DSTS, edge, width), (DEV_BLOCKS, edge, width)
    vmem = pl.BlockSpec(memory_space=pltpu.VMEM)
    anyspace = pl.BlockSpec(memory_space=pl.ANY)
    f32 = functools.partial(jax.ShapeDtypeStruct, dtype=jnp.float32)
    sent = jnp.float32 if phase == SPLIT[0] else jnp.bfloat16
    out_shape = (f32(part), jax.ShapeDtypeStruct(part, sent)) if phase in SPLIT else (f32(whole),)
    count = GROUP * PHASE_GROUPS[phase]
    blocks = [piece.reshape(-1, edge, width) for piece in pieces]
    counts = [piece.shape[0] // DEV_BLOCKS for piece in blocks]
    slots = STEP * GROUP_STEPS * PHASE_GROUPS[phase] // 2
    results = pl.pallas_call(
        functools.partial(phase_kernel, phase, counts),
        out_shape=out_shape,
        grid_spec=pltpu.PrefetchScalarGridSpec(
            num_scalar_prefetch=1,
            grid=(),
            in_specs=[anyspace] * (1 + len(blocks)) + ([vmem] if phase else []),
            out_specs=(vmem,) * len(out_shape),
            scratch_shapes=[
                pltpu.VMEM((1 + count * DEV_BLOCKS, edge, width), pieces[0].dtype),
                pltpu.VMEM((count * OWNER_TILES, edge, edge), tiles.dtype),
                pltpu.VMEM(whole, jnp.float32),
                pltpu.SemaphoreType.DMA((PHASE_GROUPS[phase],)),
            ],
        ),
        compiler_params=pltpu.CompilerParams(vmem_limit_bytes=VMEM_BYTES),
        cost_estimate=pl.CostEstimate(
            flops=slots * 128 * 128 * 256 * 2, bytes_accessed=slots * 32 * 1024, transcendentals=0
        ),
        name="phase",
    )(meta, tiles, *blocks, *((before,) if phase else ()))
    return results if len(results) > 1 else results[0]


def both(pieces):
    return list(pieces) + [send(rows, shift(c=1)) for rows in pieces]


def on_device(
    features, tile_vals, tile_dst, tile_src, tile_count, degree, w_self, w_neigh, out_bias
):
    row, rep = lax.axis_index("row"), lax.axis_index("rep")
    swap = [(0, 1), (1, 0)]
    hold = lax.optimization_barrier
    from_minus = send(features, along_first(1))
    from_plus = send(features, along_first(-1))
    from_far = send(features, along_first(2))
    across = send(features, shift(x=1))
    listed, starts, fills, steps = work_list(tile_dst, tile_src, tile_count[0], row)
    meta = []
    for base, groups in zip(GROUP_BASE, PHASE_GROUPS):
        parts = [
            lax.slice_in_dim(values, base * size, (base + groups) * size)
            for values, size in ((listed, GROUP_STEPS * STEP), (starts, GROUP), (fills, GROUP), (steps, 1))
        ]
        meta.append(jnp.concatenate(parts + [rep[None]]).astype(jnp.int32))
    from_minus, from_plus, from_far, across, meta = hold((from_minus, from_plus, from_far, across, meta))
    line = jnp.concatenate([features, from_minus, from_plus, from_far])
    rest = send(line[DEV_ROWS:], shift(x=1))
    minus = send(line, along_second(1))
    plus = send(line, along_second(-1))
    total = run_phase(0, meta[0], tile_vals, both((line,)))
    minus, plus, total = hold((minus, plus, total))
    far_head = send(minus[: 2 * DEV_ROWS], along_second(1))
    far_tail = send(plus[2 * DEV_ROWS :], along_second(-1))
    near_siblings = both((minus, plus))[2:]
    other = jnp.concatenate([across, rest])
    other_minus = send(other, along_second(1))
    other_plus = send(other, along_second(-1))
    far_siblings = both((far_head, far_tail))[2:]

    pieces = [minus, plus, far_head, far_tail] + near_siblings + far_siblings
    near, away = run_phase(1, meta[1], tile_vals, pieces, total)
    early = lax.ppermute(away, "rep", swap)
    other_minus, other_plus, near = hold((other_minus, other_plus, near))
    last_head = send(other_minus[: 2 * DEV_ROWS], along_second(1))
    last_tail = send(other_plus[2 * DEV_ROWS :], along_second(-1))

    total = run_phase(2, meta[2], tile_vals, both((other, other_minus, other_plus)), near)
    last_head, last_tail, total = hold((last_head, last_tail, total))
    last = both((last_head, last_tail))
    total, early = hold((total, early))
    near, away = run_phase(3, meta[3], tile_vals, last, total)
    late = lax.ppermute(away, "rep", swap)
    summed = (near + early + late.astype(jnp.float32)).reshape(features.shape)
    neighbours = (summed / jnp.sqrt(degree.astype(jnp.float32))[:, None]).astype(jnp.bfloat16)
    mixed = jnp.dot(features, w_self, preferred_element_type=jnp.float32) + out_bias[None, :]
    mixed = mixed + jnp.dot(neighbours, w_neigh, preferred_element_type=jnp.float32)
    return jnp.maximum(mixed, 0.0).astype(jnp.bfloat16)


def solution(mesh):
    in_specs = (
        P(("rep", "row"), None),
        P(("rep", "row"), None, None),
        P(("rep", "row")),
        P(("rep", "row")),
        P(("rep", "row")),
        P(("rep", "row")),
        P(),
        P(),
        P(),
    )
    out_specs = P(("rep", "row"), None)
    return jax.shard_map(
        on_device, mesh=mesh, in_specs=in_specs, out_specs=out_specs, check_vma=False
    )
```
